32 devices in a mesh: grp: 2 (over x), row: 8 (over z, y), col: 2 (over core).
Axes of the slice: x: 2, y: 2, z: 4, core: 2. Of those that a mesh axis runs over, the one named last changes fastest.
Arguments:
- tiles: float32 [3072, 128, 128], P(('grp', 'row', 'col')), parts along dimension 0, as said below
- tile_rows: int32 [3072], P(('grp', 'row', 'col')), parts along dimension 0, may hold values from 0 to 15, as said below
- tile_cols: int32 [3072], P(('grp', 'row', 'col')), parts along dimension 0, may hold values from 0 to 127, as said below
- counts: int32 [32], P(('grp', 'row', 'col')), parts along dimension 0, may hold values from 32 to 96, as said below
- cost: float32 [65536], P(('grp', 'col')), parts along dimension 0, may hold values from -6 to 6
- lower: float32 [65536], P(('grp', 'col')), parts along dimension 0, may hold values from -1.5 to -0.1
- upper: float32 [65536], P(('grp', 'col')), parts along dimension 0, may hold values from 0.1 to 1.5
- rhs: float32 [32768], P(('grp', 'row')), parts along dimension 0, may hold values from -6 to 6
- primal_start: float32 [65536], P(('grp', 'col')), parts along dimension 0, may hold values from -3 to 3
- dual_start: float32 [32768], P(('grp', 'row')), parts along dimension 0, may hold values from 0 to 1
- step_start: float32 [2], P('grp'), parts along dimension 0, may hold values from 0.3 to 0.6
Outputs:
- primal_solution: float32 [65536], P(('grp', 'col')), parts along dimension 0
- dual_solution: float32 [32768], P(('grp', 'row')), parts along dimension 0
- row_scaling: float32 [32768], P(('grp', 'row')), parts along dimension 0
- column_scaling: float32 [65536], P(('grp', 'col')), parts along dimension 0
- step_taken: float32 [2], P('grp'), parts along dimension 0
The draws below stay inside these ranges and needn't reach their ends.
There are 2 independent parts, one for each index of `grp`. The reference program is written for one: setup_inputs(seed, part) draws one part's arguments, and reference() takes and returns one part's arrays. A program takes and returns all parts, laid end to end along the dimension named above; each array names one. Nothing has to cross between parts.
Inputs may be any that keep to these rules, and one draw needn't show every extreme that they name: `tile_rows`: every tile row of the program holds at least one live tile. `tile_cols`: every tile column of the program holds at least one live tile. A device's live tiles are its first counts slots; some device has all 96 slots live in every draw. `tiles`: entries of the slots; those past a device's count are not part of the matrix.
All inputs are finite; a program needn't handle non-finite values.
Results may differ from the reference program's by a relative error of at most 0.00022.
Values sent between devices are 32-bit elements; how exact they have to be, the bound alone decides.
A program may use at most 64 MiB of HBM per device.

```python
import math
import jax
import jax.numpy as jnp
from jax import lax

TILE = 128
RB_DEV = 16
COL_DEV = 16
RUIZ = 4
ITERS = 2
CB_DEV = 128
CAP = 96
SLOTS = 1536
ROWS = 16384
COLS = 32768
N_ROW = 8
N_COL = 2


def tile_layout(key):
    base_slots = COL_DEV + RB_DEV
    device_total = N_ROW * N_COL
    device_keys = jax.random.split(key, device_total)

    def one_device(device_key, device_id):
        row_device = device_id // N_COL
        key_rows, key_cols, key_order = jax.random.split(device_key, 3)
        random_rows = jax.random.randint(key_rows, (CAP,), 0, RB_DEV)
        random_cols = jax.random.randint(key_cols, (CAP,), 0, CB_DEV)
        slot_index = jnp.arange(CAP)
        cover_cols = slot_index * N_ROW + row_device
        cover_rows = slot_index - COL_DEV
        row_index = jnp.where((slot_index >= COL_DEV) & (slot_index < base_slots), cover_rows, random_rows)
        col_index = jnp.where(slot_index < COL_DEV, cover_cols, random_cols)
        ordering = jnp.concatenate([jax.random.permutation(key_order, base_slots), jnp.arange(base_slots, CAP)])
        return (row_index[ordering], col_index[ordering])
    row_index, col_index = jax.vmap(one_device)(device_keys, jnp.arange(device_total))
    return (row_index.reshape(-1).astype(jnp.int32), col_index.reshape(-1).astype(jnp.int32))


def draw_tile_rows(key, part):
    return tile_layout(key)[0]


def draw_tile_cols(key, part):
    return tile_layout(key)[1]


def draw_counts(key, part):
    key = jax.random.fold_in(key, 5)
    key_level, key_top = jax.random.split(key)
    device_total = N_ROW * N_COL
    base_slots = COL_DEV + RB_DEV
    spare = CAP - base_slots
    levels = jax.random.randint(key_level, (device_total,), 0, spare + 1)
    fullest = jax.random.randint(key_top, (), 0, device_total)
    levels = jnp.where(jnp.arange(device_total) == fullest, spare, levels)
    return (base_slots + levels * levels * levels // (spare * spare)).astype(jnp.int32)


def draw_tiles(key, part):
    key = jax.random.fold_in(key, 7)
    key_base, key_left, key_right = jax.random.split(key, 3)
    shape_all = (SLOTS, TILE, TILE)
    values = jax.random.normal(key_base, shape_all, jnp.float32)
    spread = math.log(10.0)
    left_factor = jnp.exp(jax.random.uniform(key_left, (SLOTS, TILE, 1), jnp.float32) * spread)
    right_factor = jnp.exp(jax.random.uniform(key_right, (SLOTS, 1, TILE), jnp.float32) * spread)
    return values * left_factor * right_factor


def shard_levels(stream_key, extent, cuts, least, largest):
    level, own = 1.0, jax.random.fold_in(stream_key, 6)
    for dim, shards_of in cuts:
        heights = jnp.exp(jax.random.uniform(jax.random.fold_in(own, dim), (shards_of,), jnp.float32, least / len(cuts), largest / len(cuts)))
        level = level * jnp.repeat(heights, extent[dim] // shards_of).reshape([-1 if axis == dim else 1 for axis in range(len(extent))])
    return level


def bell_draw(key, dims, deviation, most, cuts=(), held_as=jnp.bfloat16):
    array = jax.random.normal(key, dims, jnp.float32) * deviation
    if len(cuts) > 0:
        array = shard_levels(key, dims, cuts, -0.22, 0.18) * array
    return jnp.clip(array, min=-most, max=most).astype(held_as)


def setup_inputs(seed: int = 0, part: int = 0) -> dict:
    key_of = jax.random.split(jax.random.key(seed), 12)
    own_keys = jax.random.split(jax.random.fold_in(key_of[11], part), 12)
    return {
        "tiles": draw_tiles(jax.random.fold_in(jax.random.fold_in(key_of[11], part), 71), part),
        "tile_rows": draw_tile_rows(jax.random.fold_in(jax.random.fold_in(key_of[11], part), 71), part),
        "tile_cols": draw_tile_cols(jax.random.fold_in(jax.random.fold_in(key_of[11], part), 71), part),
        "counts": draw_counts(jax.random.fold_in(jax.random.fold_in(key_of[11], part), 71), part),
        "cost": bell_draw(own_keys[4], (COLS,), 1.0, 6.0, ((0, 2),), jnp.float32),
        "lower": jnp.clip(-1.5 + 1.4 * jax.random.uniform(own_keys[5], (COLS,), jnp.float32) ** shard_levels(own_keys[5], (COLS,), ((0, 2),), -0.2, 0.2), -1.5, -0.1),
        "upper": jnp.clip(0.1 + 1.4 * jax.random.uniform(own_keys[6], (COLS,), jnp.float32) ** shard_levels(own_keys[6], (COLS,), ((0, 2),), -0.2, 0.2), 0.1, 1.5),
        "rhs": bell_draw(own_keys[7], (ROWS,), 1.0, 6.0, ((0, 8),), jnp.float32),
        "primal_start": bell_draw(own_keys[8], (COLS,), 0.5, 3.0, ((0, 2),), jnp.float32),
        "dual_start": jnp.clip(1.0 * jax.random.uniform(own_keys[9], (ROWS,), jnp.float32) ** shard_levels(own_keys[9], (ROWS,), ((0, 8),), -0.2, 0.2), 0.0, 1.0),
        "step_start": jnp.clip(jax.random.uniform(own_keys[10], (1,), jnp.float32, 0.3, 0.6), 0.3, 0.6),
    }


EPS = 1e-06

def slot_layout(tile_rows, tile_cols, counts):
    slot_index = jnp.arange(tile_rows.shape[0], dtype=jnp.int32)
    device_of = slot_index // CAP
    row_block = device_of // N_COL * RB_DEV + tile_rows
    col_block = device_of % N_COL * CB_DEV + tile_cols
    live_slots = slot_index % CAP < counts[device_of]
    return (row_block, col_block, live_slots)

def forward_product(tiles, row_block, col_block, live_slots, vector):
    pieces = vector.reshape(-1, TILE)[col_block]
    product = jnp.einsum('sij,sj->si', tiles, pieces, precision=lax.Precision.HIGHEST)
    product = jnp.where(live_slots[:, None], product, 0.0)
    return jax.ops.segment_sum(product, row_block, num_segments=RB_DEV * N_ROW).reshape(-1)

def backward_product(tiles, row_block, col_block, live_slots, vector):
    pieces = vector.reshape(-1, TILE)[row_block]
    product = jnp.einsum('sij,si->sj', tiles, pieces, precision=lax.Precision.HIGHEST)
    product = jnp.where(live_slots[:, None], product, 0.0)
    return jax.ops.segment_sum(product, col_block, num_segments=CB_DEV * N_COL).reshape(-1)

def reference(tiles, tile_rows, tile_cols, counts, cost, lower, upper, rhs, primal_start, dual_start, step_start):
    row_block, col_block, live_slots = slot_layout(tile_rows, tile_cols, counts)
    magnitude = jnp.abs(tiles)
    row_scale = jnp.ones_like(rhs)
    col_scale = jnp.ones_like(cost)
    for sweep in range(RUIZ):
        col_pieces = col_scale.reshape(-1, TILE)[col_block]
        row_pieces = row_scale.reshape(-1, TILE)[row_block]
        row_part = jnp.where(live_slots[:, None], lax.optimization_barrier(jnp.max(magnitude * col_pieces[:, None, :], axis=2)), 0.0)
        col_part = jnp.where(live_slots[:, None], lax.optimization_barrier(jnp.max(magnitude * row_pieces[:, :, None], axis=1)), 0.0)
        row_peak = jax.ops.segment_max(row_part, row_block, num_segments=RB_DEV * N_ROW).reshape(-1) * row_scale
        col_peak = jax.ops.segment_max(col_part, col_block, num_segments=CB_DEV * N_COL).reshape(-1) * col_scale
        row_scale = row_scale / jnp.sqrt(row_peak + EPS)
        col_scale = col_scale / jnp.sqrt(col_peak + EPS)
    cost_scaled = col_scale * cost
    rhs_scaled = row_scale * rhs
    lower_scaled = lower / col_scale
    upper_scaled = upper / col_scale
    primal = primal_start / col_scale
    dual_vec = dual_start / row_scale
    weight_ratio = jnp.sqrt(jnp.sum(cost_scaled * cost_scaled) + EPS) / jnp.sqrt(jnp.sum(rhs_scaled * rhs_scaled) + EPS)
    step_size = step_start[0]

    def apply_matrix(vector):
        return row_scale * forward_product(tiles, row_block, col_block, live_slots, col_scale * vector)
    image_now = apply_matrix(primal)
    for iteration in range(ITERS):
        gradient = col_scale * backward_product(tiles, row_block, col_block, live_slots, row_scale * dual_vec)
        primal_next = jnp.clip(primal - step_size / weight_ratio * (cost_scaled - gradient), lower_scaled, upper_scaled)
        image_next = apply_matrix(primal_next)
        dual_next = jnp.maximum(dual_vec + step_size * weight_ratio * (rhs_scaled - 2.0 * image_next + image_now), 0.0)
        primal_move = primal_next - primal
        dual_move = dual_next - dual_vec
        primal_sq = jnp.sum(primal_move * primal_move)
        dual_sq = jnp.sum(dual_move * dual_move)
        coupling = jnp.sum(dual_move * (image_next - image_now))
        movement = 0.5 * weight_ratio * primal_sq + 0.5 / weight_ratio * dual_sq + EPS
        growth = (1.0 + (iteration + 2.0) ** (-0.6)) * step_size
        limit_term = (1.0 - (iteration + 2.0) ** (-0.3)) * movement
        step_size = limit_term / jnp.maximum(jnp.abs(coupling), limit_term / growth)
        primal, dual_vec, image_now = (primal_next, dual_next, image_next)
    return (col_scale * primal, row_scale * dual_vec, row_scale, col_scale, jnp.reshape(step_size, (1,)))
```

```python
import functools

import jax
import jax.numpy as jnp
from jax import lax
from jax.experimental import pallas as pl
from jax.experimental.pallas import tpu as pltpu
from jax.sharding import PartitionSpec as P

RUIZ = 4
ITERS = 2
EPS = 1e-06
MESH = pl.DeviceIdType.MESH
SIDE = 8


def kernel(
    n_row,
    n_col,
    tr_ref,
    tc_ref,
    count_ref,
    step_ref,
    tiles_ref,
    cost_ref,
    lower_ref,
    upper_ref,
    rhs_ref,
    primal_ref,
    dual_ref,
    primal_out,
    dual_out,
    rscale_out,
    cscale_out,
    step_out,
    rowmat,
    colvec,
    colpart,
    rowpart,
    rs_send,
    rs_recv,
    ag_recv,
    pair_recv,
    last_recv,
    rs_ssem,
    rs_rsem,
    ag_ssem,
    ag_rsem,
    pair_ssem,
    pair_rsem,
    last_ssem,
    last_rsem,
):
    slots, tile, _ = tiles_ref.shape
    row_blocks = rhs_ref.shape[0]
    col_blocks = cost_ref.shape[0]
    own = col_blocks // n_row
    unroll = next(u for u in (8, 4, 2, 1) if slots % u == 0)
    grp = lax.axis_index("grp")
    me = lax.axis_index("row")
    core = lax.axis_index("col")
    mine = pl.ds(pl.multiple_of(me * own, own), own)
    count = count_ref[0]

    barrier = pltpu.get_barrier_semaphore()

    def greet(step, _):
        peer = lax.rem(me + step, n_row)
        pl.semaphore_signal(barrier, inc=1, device_id=(grp, peer, core), device_id_type=MESH)
        return 0

    lax.fori_loop(1, n_row, greet, 0)
    for step in range(1, n_col):
        peer = lax.rem(core + step, n_col)
        pl.semaphore_signal(barrier, inc=1, device_id=(grp, me, peer), device_id_type=MESH)

    def over_peers(act):
        def body(step, _):
            act(lax.rem(me + step, n_row))
            return 0

        lax.fori_loop(1, n_row, body, 0)

    def rs_copy(k, peer, source):
        return pltpu.make_async_remote_copy(
            src_ref=rs_send.at[k, peer],
            dst_ref=rs_recv.at[k, source],
            send_sem=rs_ssem.at[k, peer],
            recv_sem=rs_rsem.at[k, source],
            device_id=(grp, peer, core),
            device_id_type=MESH,
        )

    def ag_copy(k, peer, source):
        return pltpu.make_async_remote_copy(
            src_ref=ag_recv.at[k, source],
            dst_ref=ag_recv.at[k, source],
            send_sem=ag_ssem.at[k, peer],
            recv_sem=ag_rsem.at[k, source],
            device_id=(grp, peer, core),
            device_id_type=MESH,
        )

    def last_copy(peer, source):
        return pltpu.make_async_remote_copy(
            src_ref=last_recv.at[source],
            dst_ref=last_recv.at[source],
            send_sem=last_ssem.at[peer],
            recv_sem=last_rsem.at[source],
            device_id=(grp, peer, core),
            device_id_type=MESH,
        )

    def pair_copy(k, peer, source):
        return pltpu.make_async_remote_copy(
            src_ref=pair_recv.at[k, source],
            dst_ref=pair_recv.at[k, source],
            send_sem=pair_ssem.at[k, peer],
            recv_sem=pair_rsem.at[k, source],
            device_id=(grp, me, peer),
            device_id_type=MESH,
        )

    def send_pair(k, value, side):
        pair_recv[k, core, 0:row_blocks] = value
        pair_recv[k, core, row_blocks : row_blocks + SIDE] = jnp.broadcast_to(side, (SIDE, tile))
        for step in range(1, n_col):
            pair_copy(k, lax.rem(core + step, n_col), core).start()

    def take_pair(k, combine):
        for step in range(1, n_col):
            peer = lax.rem(core + step, n_col)
            pair_copy(k, peer, peer).wait_recv()
        value = pair_recv[k, 0, 0:row_blocks]
        side = pair_recv[k, 0, row_blocks : row_blocks + SIDE]
        for c in range(1, n_col):
            value = combine(value, pair_recv[k, c, 0:row_blocks])
            side = side + pair_recv[k, c, row_blocks : row_blocks + SIDE]
        return value, side

    def scatter_cols(k, combine, side):
        ids = lax.broadcasted_iota(jnp.int32, (own, tile), 0)

        def owner(p, _):
            first = p * own

            def group(i, total):
                for u in range(unroll):
                    s = i * unroll + u
                    at = jnp.where(s < count, tc_ref[s] - first, -1)
                    part = colpart[pl.ds(s, 1), :]
                    total = combine(total, jnp.where(ids == at, part, 0.0))
                return total

            total = lax.fori_loop(
                0, slots // unroll, group, jnp.zeros((own, tile), jnp.float32)
            )
            rs_send[k, p, 0:own] = total
            rs_send[k, p, own : own + SIDE] = jnp.broadcast_to(side, (SIDE, tile))
            return 0

        lax.fori_loop(0, n_row, owner, 0)
        rs_recv[k, me] = rs_send[k, me]

    def send_rs(k):
        over_peers(lambda peer: rs_copy(k, peer, me).start())

    def take_rs(k, combine):
        over_peers(lambda peer: rs_copy(k, peer, peer).wait_recv())
        value = rs_recv[k, 0, 0:own]
        side = rs_recv[k, 0, own : own + SIDE]
        for p in range(1, n_row):
            value = combine(value, rs_recv[k, p, 0:own])
            side = side + rs_recv[k, p, own : own + SIDE]
        return value, side

    def send_ag(k, value, side):
        ag_recv[k, me, 0:own] = value
        ag_recv[k, me, own : own + SIDE] = jnp.broadcast_to(side, (SIDE, tile))
        over_peers(lambda peer: ag_copy(k, peer, me).start())

    def take_ag(k):
        over_peers(lambda peer: ag_copy(k, peer, peer).wait_recv())
        side = ag_recv[k, 0, own : own + SIDE]
        for p in range(n_row):
            colvec[p * own : (p + 1) * own, :] = ag_recv[k, p, 0:own]
            if p > 0:
                side = side + ag_recv[k, p, own : own + SIDE]
        return side

    def set_rows(vector):
        for r in range(row_blocks):
            wide = jnp.broadcast_to(vector[r : r + 1, :], (tile, tile))
            rowmat[r] = jnp.transpose(wide)

    def col_pass(reduce, transform):
        def group(i, _):
            for u in range(unroll):
                s = i * unroll + u
                block = transform(tiles_ref[s] * rowmat[tr_ref[s]])
                colpart[pl.ds(s, 1), :] = reduce(block, axis=0, keepdims=True)
            return 0

        lax.fori_loop(0, slots // unroll, group, 0)

    def row_pass(reduce, transform, combine):
        lanes = lax.broadcasted_iota(jnp.int32, (tile, tile), 1)

        def group(i, total):
            for u in range(unroll):
                s = i * unroll + u
                block = transform(tiles_ref[s] * colvec[pl.ds(tc_ref[s], 1), :])
                total = jnp.where(lanes == s, reduce(block, axis=1, keepdims=True), total)
            return total

        total = lax.fori_loop(
            0, slots // unroll, group, jnp.zeros((tile, tile), jnp.float32)
        )
        rowpart[...] = jnp.transpose(total)
        ids = lax.broadcasted_iota(jnp.int32, (row_blocks, tile), 0)

        def place(i, total):
            for u in range(unroll):
                s = i * unroll + u
                at = jnp.where(s < count, tr_ref[s], -1)
                part = rowpart[pl.ds(s, 1), :]
                total = combine(total, jnp.where(ids == at, part, 0.0))
            return total

        return lax.fori_loop(
            0, slots // unroll, place, jnp.zeros((row_blocks, tile), jnp.float32)
        )

    def plain(block):
        return block

    add = jnp.add
    none = jnp.zeros((1, tile), jnp.float32)

    def total_of(value):
        part = jnp.sum(jnp.sum(value, axis=0, keepdims=True), axis=1, keepdims=True)
        return jnp.broadcast_to(part, (1, tile))

    row_scale = jnp.ones((row_blocks, tile), jnp.float32)
    col_scale = jnp.ones((own, tile), jnp.float32)
    colvec[...] = jnp.ones((col_blocks, tile), jnp.float32)
    for sweep in range(RUIZ):
        set_rows(row_scale)
        col_pass(jnp.max, jnp.abs)
        scatter_cols(sweep, jnp.maximum, none)
        if sweep == 0:
            pl.semaphore_wait(barrier, n_row + n_col - 2)
        send_rs(sweep)
        if sweep > 0:
            take_ag(sweep - 1)
        row_local = row_pass(jnp.max, jnp.abs, jnp.maximum)
        send_pair(sweep, row_local, none)
        col_peak = take_rs(sweep, jnp.maximum)[0] * col_scale
        col_scale = col_scale / jnp.sqrt(col_peak + EPS)
        send_ag(sweep, col_scale, none)
        row_peak = take_pair(sweep, jnp.maximum)[0] * row_scale
        row_scale = row_scale / jnp.sqrt(row_peak + EPS)

    rscale_out[...] = row_scale
    rhs_scaled = row_scale * rhs_ref[...]
    dual = dual_ref[...] / row_scale
    set_rows(row_scale * dual)
    col_pass(jnp.sum, plain)
    scatter_cols(RUIZ, add, total_of(rhs_scaled * rhs_scaled))
    send_rs(RUIZ)

    take_ag(RUIZ - 1)
    whole_scale = colvec[...]
    cscale_out[...] = whole_scale
    whole_cost = whole_scale * cost_ref[...]
    colvec[...] = whole_scale * (primal_ref[...] / whole_scale)
    send_pair(RUIZ, row_pass(jnp.sum, plain, add), total_of(whole_cost * whole_cost))

    cost_scaled = col_scale * cost_ref[mine, :]
    lower_scaled = lower_ref[mine, :] / col_scale
    upper_scaled = upper_ref[mine, :] / col_scale
    primal = primal_ref[mine, :] / col_scale
    eta = jnp.full((1, tile), step_ref[0], jnp.float32)

    side_rows = lax.broadcasted_iota(jnp.int32, (SIDE, tile), 0)
    weight = None
    image = None
    before = None
    for k in range(ITERS):
        gradient, side = take_rs(RUIZ + k, add)
        gradient = col_scale * gradient
        if k == 0:
            image, cost_side = take_pair(RUIZ, add)
            image = row_scale * image
            weight = jnp.sqrt(cost_side[0:1] + EPS) / jnp.sqrt(side[0:1] + EPS)
        else:
            eta = next_step(k - 1, eta, weight, before, side)
        primal_next = jnp.clip(
            primal - eta / weight * (cost_scaled - gradient), lower_scaled, upper_scaled
        )
        moved = primal_next - primal
        send_ag(RUIZ + k, col_scale * primal_next, total_of(moved * moved))
        primal = primal_next
        moved_sq = take_ag(RUIZ + k)[0:1]
        send_pair(RUIZ + 1 + k, row_pass(jnp.sum, plain, add), moved_sq)
        image_next, before = take_pair(RUIZ + 1 + k, add)
        before = before[0:1]
        image_next = row_scale * image_next
        dual_next = jnp.maximum(
            dual + eta * weight * (rhs_scaled - 2.0 * image_next + image), 0.0
        )
        moved = dual_next - dual
        both = jnp.where(
            side_rows == 0,
            total_of(moved * moved),
            total_of(moved * (image_next - image)),
        )
        dual, image = dual_next, image_next
        if k < ITERS - 1:
            set_rows(row_scale * dual)
            col_pass(jnp.sum, plain)
            scatter_cols(RUIZ + 1 + k, add, both)
            send_rs(RUIZ + 1 + k)
        else:
            last_recv[me] = both
            over_peers(lambda peer: last_copy(peer, me).start())
            primal_out[...] = colvec[...]
            dual_out[...] = row_scale * dual
            over_peers(lambda peer: last_copy(peer, peer).wait_recv())
            side = last_recv[0]
            for p in range(1, n_row):
                side = side + last_recv[p]
            eta = next_step(k, eta, weight, before, side)
    step_out[...] = eta[:, 0:1]

    for k in range(RUIZ + ITERS):
        over_peers(lambda peer: rs_copy(k, peer, me).wait_send())
        over_peers(lambda peer: ag_copy(k, peer, me).wait_send())
    for k in range(RUIZ + ITERS + 1):
        for step in range(1, n_col):
            pair_copy(k, lax.rem(core + step, n_col), core).wait_send()
    over_peers(lambda peer: last_copy(peer, me).wait_send())


def next_step(k, eta, weight, primal_sq, side):
    dual_sq, coupling = side[0:1], side[1:2]
    movement = 0.5 * weight * primal_sq + 0.5 / weight * dual_sq + EPS
    growth = (1.0 + (k + 2.0) ** (-0.6)) * eta
    limit = (1.0 - (k + 2.0) ** (-0.3)) * movement
    return limit / jnp.maximum(jnp.abs(coupling), limit / growth)


def body(
    n_row,
    n_col,
    tiles,
    tile_rows,
    tile_cols,
    counts,
    cost,
    lower,
    upper,
    rhs,
    primal_start,
    dual_start,
    step_start,
):
    slots, tile, _ = tiles.shape
    row_blocks = rhs.shape[0] // tile
    col_blocks = cost.shape[0] // tile
    own = col_blocks // n_row
    phases = RUIZ + ITERS
    smem = pl.BlockSpec(memory_space=pltpu.SMEM)
    vmem = pl.BlockSpec(memory_space=pltpu.VMEM)
    f32 = jnp.float32

    def cols(x):
        return x.reshape(col_blocks, tile)

    def rows(x):
        return x.reshape(row_blocks, tile)

    dma = pltpu.SemaphoreType.DMA
    primal, dual, row_scale, col_scale, step = pl.pallas_call(
        functools.partial(kernel, n_row, n_col),
        out_shape=(
            jax.ShapeDtypeStruct((col_blocks, tile), f32),
            jax.ShapeDtypeStruct((row_blocks, tile), f32),
            jax.ShapeDtypeStruct((row_blocks, tile), f32),
            jax.ShapeDtypeStruct((col_blocks, tile), f32),
            jax.ShapeDtypeStruct((1, 1), f32),
        ),
        in_specs=[smem] * 4 + [vmem] * 7,
        out_specs=(vmem,) * 5,
        scratch_shapes=[
            pltpu.VMEM((row_blocks, tile, tile), f32),
            pltpu.VMEM((col_blocks, tile), f32),
            pltpu.VMEM((slots, tile), f32),
            pltpu.VMEM((tile, tile), f32),
            pltpu.VMEM((phases, n_row, own + SIDE, tile), f32),
            pltpu.VMEM((phases, n_row, own + SIDE, tile), f32),
            pltpu.VMEM((phases, n_row, own + SIDE, tile), f32),
            pltpu.VMEM((phases + 1, n_col, row_blocks + SIDE, tile), f32),
            pltpu.VMEM((n_row, SIDE, tile), f32),
            dma((phases, n_row)),
            dma((phases, n_row)),
            dma((phases, n_row)),
            dma((phases, n_row)),
            dma((phases + 1, n_col)),
            dma((phases + 1, n_col)),
            dma((n_row,)),
            dma((n_row,)),
        ],
        compiler_params=pltpu.CompilerParams(
            collective_id=0, has_side_effects=True, vmem_limit_bytes=40 * 1024 * 1024
        ),
        name="equilibrate_and_iterate",
    )(
        tile_rows,
        tile_cols,
        counts,
        step_start,
        tiles,
        cols(cost),
        cols(lower),
        cols(upper),
        rows(rhs),
        cols(primal_start),
        rows(dual_start),
    )
    return (
        primal.reshape(-1),
        dual.reshape(-1),
        row_scale.reshape(-1),
        col_scale.reshape(-1),
        step.reshape(-1),
    )


def solution(mesh):
    in_specs = (
        P(("grp", "row", "col"), None, None),
        P(("grp", "row", "col")),
        P(("grp", "row", "col")),
        P(("grp", "row", "col")),
        P(("grp", "col")),
        P(("grp", "col")),
        P(("grp", "col")),
        P(("grp", "row")),
        P(("grp", "col")),
        P(("grp", "row")),
        P("grp"),
    )
    out_specs = (
        P(("grp", "col")),
        P(("grp", "row")),
        P(("grp", "row")),
        P(("grp", "col")),
        P("grp"),
    )
    local = functools.partial(body, mesh.shape["row"], mesh.shape["col"])
    return jax.shard_map(local, mesh=mesh, in_specs=in_specs, out_specs=out_specs, check_vma=False)
```

```python
import functools

import jax
import jax.numpy as jnp
from jax import lax
from jax.experimental import pallas as pl
from jax.experimental.pallas import tpu as pltpu
from jax.sharding import PartitionSpec as P

RUIZ = 4
ITERS = 2
EPS = 1e-06
MESH = pl.DeviceIdType.MESH
SIDE = 8


def kernel(
    n_row,
    n_col,
    count_ref,
    step_ref,
    tr_hbm,
    tc_hbm,
    tiles_hbm,
    cost_hbm,
    lower_hbm,
    upper_hbm,
    rhs_hbm,
    primal_hbm,
    dual_hbm,
    primal_out,
    dual_out,
    rscale_out,
    cscale_out,
    step_out,
    tr_ref,
    tc_ref,
    tiles_ref,
    cost_ref,
    lower_ref,
    upper_ref,
    rhs_ref,
    primal_ref,
    dual_ref,
    load_sem,
    tile_sem,
    listed,
    order,
    order_sem,
    keycol,
    running,
    rowmat,
    colvec,
    colpart,
    rs_send,
    rs_recv,
    ag_recv,
    pair_recv,
    last_recv,
    rs_ssem,
    rs_rsem,
    ag_ssem,
    ag_rsem,
    pair_ssem,
    pair_rsem,
    last_ssem,
    last_rsem,
):
    slots, tile, _ = tiles_ref.shape
    row_blocks = rhs_ref.shape[0]
    col_blocks = cost_ref.shape[0]
    own = col_blocks // n_row
    unroll = next(u for u in (8, 4, 2, 1) if slots % u == 0)
    grp = lax.axis_index("grp")
    me = lax.axis_index("row")
    core = lax.axis_index("col")
    mine = pl.ds(pl.multiple_of(me * own, own), own)
    count = count_ref[0]

    small = [
        pltpu.make_async_copy(source, target, load_sem.at[i])
        for i, (source, target) in enumerate(
            [
                (tr_hbm, tr_ref),
                (tc_hbm, tc_ref),
                (cost_hbm, cost_ref),
                (lower_hbm, lower_ref),
                (upper_hbm, upper_ref),
                (rhs_hbm, rhs_ref),
                (primal_hbm, primal_ref),
                (dual_hbm, dual_ref),
            ]
        )
    ]

    def tile_copy(i):
        some = pl.ds(i * unroll, unroll)
        return pltpu.make_async_copy(tiles_hbm.at[some], tiles_ref.at[some], tile_sem.at[i])

    def load_tiles(i, _):
        tile_copy(i).start()
        return 0

    small[0].start()
    small[1].start()
    lax.fori_loop(0, slots // unroll, load_tiles, 0)
    for copy in small[2:]:
        copy.start()

    barrier = pltpu.get_barrier_semaphore()

    def greet(step, _):
        peer = lax.rem(me + step, n_row)
        pl.semaphore_signal(barrier, inc=1, device_id=(grp, peer, core), device_id_type=MESH)
        return 0

    lax.fori_loop(1, n_row, greet, 0)
    for step in range(1, n_col):
        peer = lax.rem(core + step, n_col)
        pl.semaphore_signal(barrier, inc=1, device_id=(grp, me, peer), device_id_type=MESH)

    def over_peers(act):
        def body(step, _):
            act(lax.rem(me + step, n_row))
            return 0

        lax.fori_loop(1, n_row, body, 0)

    def length(k):
        return own if k < RUIZ else own + SIDE

    def rs_copy(k, peer, source):
        return pltpu.make_async_remote_copy(
            src_ref=rs_send.at[k, peer, pl.ds(0, length(k))],
            dst_ref=rs_recv.at[k, source, pl.ds(0, length(k))],
            send_sem=rs_ssem.at[k, peer],
            recv_sem=rs_rsem.at[k, source],
            device_id=(grp, peer, core),
            device_id_type=MESH,
        )

    def ag_copy(k, peer, source):
        return pltpu.make_async_remote_copy(
            src_ref=ag_recv.at[k, source, pl.ds(0, length(k))],
            dst_ref=ag_recv.at[k, source, pl.ds(0, length(k))],
            send_sem=ag_ssem.at[k, peer],
            recv_sem=ag_rsem.at[k, source],
            device_id=(grp, peer, core),
            device_id_type=MESH,
        )

    def last_copy(peer, source):
        return pltpu.make_async_remote_copy(
            src_ref=last_recv.at[source],
            dst_ref=last_recv.at[source],
            send_sem=last_ssem.at[peer],
            recv_sem=last_rsem.at[source],
            device_id=(grp, peer, core),
            device_id_type=MESH,
        )

    def pair_copy(k, peer, source):
        return pltpu.make_async_remote_copy(
            src_ref=pair_recv.at[k, source],
            dst_ref=pair_recv.at[k, source],
            send_sem=pair_ssem.at[k, peer],
            recv_sem=pair_rsem.at[k, source],
            device_id=(grp, me, peer),
            device_id_type=MESH,
        )

    def send_pair(k, value, side):
        pair_recv[k, core, 0:row_blocks] = value
        pair_recv[k, core, row_blocks : row_blocks + SIDE] = jnp.broadcast_to(side, (SIDE, tile))
        for step in range(1, n_col):
            pair_copy(k, lax.rem(core + step, n_col), core).start()

    def take_pair(k, combine):
        for step in range(1, n_col):
            peer = lax.rem(core + step, n_col)
            pair_copy(k, peer, peer).wait_recv()
        value = pair_recv[k, 0, 0:row_blocks]
        side = pair_recv[k, 0, row_blocks : row_blocks + SIDE]
        for c in range(1, n_col):
            value = combine(value, pair_recv[k, c, 0:row_blocks])
            side = side + pair_recv[k, c, row_blocks : row_blocks + SIDE]
        return value, side

    def scatter_cols(k, combine, side):
        owners = next(p for p in (4, 2, 1) if n_row % p == 0)
        ids = lax.broadcasted_iota(jnp.int32, (owners * own, tile), 0)

        def some(p, _):
            first = p * (owners * own)

            def group(i, total):
                for u in range(unroll):
                    s = i * unroll + u
                    at = jnp.where(s < count, tc_ref[s] - first, -1)
                    part = colpart[pl.ds(s, 1), :]
                    total = combine(total, jnp.where(ids == at, part, 0.0))
                return total

            total = lax.fori_loop(
                0, slots // unroll, group, jnp.zeros((owners * own, tile), jnp.float32)
            )
            for q in range(owners):
                rs_send[k, p * owners + q, 0:own] = total[q * own : (q + 1) * own]
                if k >= RUIZ:
                    rs_send[k, p * owners + q, own : own + SIDE] = jnp.broadcast_to(
                        side, (SIDE, tile)
                    )
            return 0

        lax.fori_loop(0, n_row // owners, some, 0)
        rs_recv[k, me, 0 : length(k)] = rs_send[k, me, 0 : length(k)]

    def send_rs(k):
        over_peers(lambda peer: rs_copy(k, peer, me).start())

    def take_rs(k, combine):
        over_peers(lambda peer: rs_copy(k, peer, peer).wait_recv())
        value = rs_recv[k, 0, 0:own]
        for p in range(1, n_row):
            value = combine(value, rs_recv[k, p, 0:own])
        if k < RUIZ:
            return value, None
        side = rs_recv[k, 0, own : own + SIDE]
        for p in range(1, n_row):
            side = side + rs_recv[k, p, own : own + SIDE]
        return value, side

    def send_ag(k, value, side):
        ag_recv[k, me, 0:own] = value
        if k >= RUIZ:
            ag_recv[k, me, own : own + SIDE] = jnp.broadcast_to(side, (SIDE, tile))
        over_peers(lambda peer: ag_copy(k, peer, me).start())

    def take_ag(k):
        over_peers(lambda peer: ag_copy(k, peer, peer).wait_recv())
        for p in range(n_row):
            colvec[p * own : (p + 1) * own, :] = ag_recv[k, p, 0:own]
        if k < RUIZ:
            return None
        side = ag_recv[k, 0, own : own + SIDE]
        for p in range(1, n_row):
            side = side + ag_recv[k, p, own : own + SIDE]
        return side

    def set_rows(vector):
        for r in range(row_blocks):
            wide = jnp.broadcast_to(vector[r : r + 1, :], (tile, tile))
            rowmat[r] = jnp.transpose(wide)

    def sort_slots():
        subs = lax.broadcasted_iota(jnp.int32, (tile, tile), 0)
        lanes = lax.broadcasted_iota(jnp.int32, (tile, tile), 1)
        lane = lax.broadcasted_iota(jnp.int32, (1, tile), 1)
        far = row_blocks + 1
        keycol[0] = jnp.full((tile, tile), far, jnp.int32)
        keys = jnp.full((1, tile), far, jnp.int32)
        for s in range(slots):
            key = jnp.where(s < count, tr_ref[s], row_blocks)
            keycol[0, s : s + 1, :] = jnp.full((1, tile), key, jnp.int32)
            keys = jnp.where(lane == s, key, keys)
        col = keycol[0]
        ahead = (col < keys) | ((col == keys) & (subs < lanes))
        listed[0, 0:1, :] = jnp.sum(ahead.astype(jnp.int32), axis=0, keepdims=True)
        copy = pltpu.make_async_copy(listed.at[0], order.at[0], order_sem.at[0])
        copy.start()
        until = jnp.sum((col <= lanes).astype(jnp.int32), axis=0, keepdims=True)
        held = jnp.sum((col == lanes).astype(jnp.int32), axis=0, keepdims=True)
        listed[1, 2:3, :] = jnp.where(held > 0, until - 1, slots)
        copy.wait()
        keycol[1] = jnp.full((tile, tile), 2 * tile, jnp.int32)
        for s in range(slots):
            keycol[1, s : s + 1, :] = jnp.full((1, tile), order[0, 0, s], jnp.int32)
        rank = keycol[1]
        here = jnp.sum(jnp.where(rank == lanes, col, 0), axis=0, keepdims=True)
        left = jnp.sum(jnp.where(rank == lanes - 1, col, 0), axis=0, keepdims=True)
        listed[1, 0:1, :] = jnp.sum(jnp.where(rank == lanes, subs, 0), axis=0, keepdims=True)
        listed[1, 1:2, :] = ((here == left) & (lane > 0)).astype(jnp.int32)
        copy = pltpu.make_async_copy(listed.at[1], order.at[1], order_sem.at[1])
        copy.start()
        running[slots] = jnp.zeros((tile, tile), jnp.float32)
        copy.wait()

    def col_pass(reduce, transform, first=False):
        def group(i, _):
            if first:
                tile_copy(i).wait()
            for u in range(unroll):
                s = i * unroll + u
                block = tiles_ref[s] if first else tiles_ref[s] * rowmat[tr_ref[s]]
                colpart[pl.ds(s, 1), :] = reduce(transform(block), axis=0, keepdims=True)
            return 0

        lax.fori_loop(0, slots // unroll, group, 0)

    def row_pass(reduce, transform, combine, first=False):
        def group(i, total):
            for u in range(unroll):
                j = i * unroll + u
                s = order[1, 0, j]
                block = tiles_ref[s]
                if not first:
                    block = block * colvec[pl.ds(tc_ref[s], 1), :]
                total = jnp.where(order[1, 1, j] == 1, total, 0.0)
                total = combine(total, transform(block))
                running[j] = total
            return total

        lax.fori_loop(0, slots // unroll, group, jnp.zeros((tile, tile), jnp.float32))
        lanes = lax.broadcasted_iota(jnp.int32, (tile, tile), 1)
        total = jnp.zeros((tile, tile), jnp.float32)
        for r in range(row_blocks):
            part = reduce(running[order[1, 2, r]], axis=1, keepdims=True)
            total = jnp.where(lanes == r, part, total)
        return jnp.transpose(total)[0:row_blocks]

    def plain(block):
        return block

    add = jnp.add
    none = jnp.zeros((1, tile), jnp.float32)

    def total_of(value):
        part = jnp.sum(jnp.sum(value, axis=0, keepdims=True), axis=1, keepdims=True)
        return jnp.broadcast_to(part, (1, tile))

    row_scale = jnp.ones((row_blocks, tile), jnp.float32)
    col_scale = jnp.ones((own, tile), jnp.float32)
    small[0].wait()
    small[1].wait()
    sort_slots()
    for sweep in range(RUIZ):
        if sweep > 0:
            set_rows(row_scale)
        col_pass(jnp.max, jnp.abs, sweep == 0)
        scatter_cols(sweep, jnp.maximum, none)
        if sweep == 0:
            pl.semaphore_wait(barrier, n_row + n_col - 2)
        send_rs(sweep)
        if sweep > 0:
            take_ag(sweep - 1)
        row_local = row_pass(jnp.max, jnp.abs, jnp.maximum, sweep == 0)
        send_pair(sweep, row_local, none)
        col_peak = take_rs(sweep, jnp.maximum)[0] * col_scale
        col_scale = col_scale / jnp.sqrt(col_peak + EPS)
        send_ag(sweep, col_scale, none)
        row_peak = take_pair(sweep, jnp.maximum)[0] * row_scale
        row_scale = row_scale / jnp.sqrt(row_peak + EPS)

    for copy in small[2:]:
        copy.wait()
    rscale_out[...] = row_scale
    rhs_scaled = row_scale * rhs_ref[...]
    dual = dual_ref[...] / row_scale
    set_rows(row_scale * dual)
    col_pass(jnp.sum, plain)
    scatter_cols(RUIZ, add, total_of(rhs_scaled * rhs_scaled))
    send_rs(RUIZ)

    take_ag(RUIZ - 1)
    whole_scale = colvec[...]
    cscale_out[...] = whole_scale
    whole_cost = whole_scale * cost_ref[...]
    colvec[...] = whole_scale * (primal_ref[...] / whole_scale)
    send_pair(RUIZ, row_pass(jnp.sum, plain, add), total_of(whole_cost * whole_cost))

    cost_scaled = col_scale * cost_ref[mine, :]
    lower_scaled = lower_ref[mine, :] / col_scale
    upper_scaled = upper_ref[mine, :] / col_scale
    primal = primal_ref[mine, :] / col_scale
    eta = jnp.full((1, tile), step_ref[0], jnp.float32)

    side_rows = lax.broadcasted_iota(jnp.int32, (SIDE, tile), 0)
    weight = None
    image = None
    before = None
    for k in range(ITERS):
        gradient, side = take_rs(RUIZ + k, add)
        gradient = col_scale * gradient
        if k == 0:
            image, cost_side = take_pair(RUIZ, add)
            image = row_scale * image
            weight = jnp.sqrt(cost_side[0:1] + EPS) / jnp.sqrt(side[0:1] + EPS)
        else:
            eta = next_step(k - 1, eta, weight, before, side)
        primal_next = jnp.clip(
            primal - eta / weight * (cost_scaled - gradient), lower_scaled, upper_scaled
        )
        moved = primal_next - primal
        send_ag(RUIZ + k, col_scale * primal_next, total_of(moved * moved))
        primal = primal_next
        moved_sq = take_ag(RUIZ + k)[0:1]
        send_pair(RUIZ + 1 + k, row_pass(jnp.sum, plain, add), moved_sq)
        image_next, before = take_pair(RUIZ + 1 + k, add)
        before = before[0:1]
        image_next = row_scale * image_next
        dual_next = jnp.maximum(
            dual + eta * weight * (rhs_scaled - 2.0 * image_next + image), 0.0
        )
        moved = dual_next - dual
        both = jnp.where(
            side_rows == 0,
            total_of(moved * moved),
            total_of(moved * (image_next - image)),
        )
        dual, image = dual_next, image_next
        if k < ITERS - 1:
            set_rows(row_scale * dual)
            col_pass(jnp.sum, plain)
            scatter_cols(RUIZ + 1 + k, add, both)
            send_rs(RUIZ + 1 + k)
        else:
            last_recv[me] = both
            over_peers(lambda peer: last_copy(peer, me).start())
            primal_out[...] = colvec[...]
            dual_out[...] = row_scale * dual
            over_peers(lambda peer: last_copy(peer, peer).wait_recv())
            side = last_recv[0]
            for p in range(1, n_row):
                side = side + last_recv[p]
            eta = next_step(k, eta, weight, before, side)
    step_out[...] = eta[:, 0:1]

    for k in range(RUIZ + ITERS):
        over_peers(lambda peer: rs_copy(k, peer, me).wait_send())
        over_peers(lambda peer: ag_copy(k, peer, me).wait_send())
    for k in range(RUIZ + ITERS + 1):
        for step in range(1, n_col):
            pair_copy(k, lax.rem(core + step, n_col), core).wait_send()
    over_peers(lambda peer: last_copy(peer, me).wait_send())


def next_step(k, eta, weight, primal_sq, side):
    dual_sq, coupling = side[0:1], side[1:2]
    movement = 0.5 * weight * primal_sq + 0.5 / weight * dual_sq + EPS
    growth = (1.0 + (k + 2.0) ** (-0.6)) * eta
    limit = (1.0 - (k + 2.0) ** (-0.3)) * movement
    return limit / jnp.maximum(jnp.abs(coupling), limit / growth)


def body(
    n_row,
    n_col,
    tiles,
    tile_rows,
    tile_cols,
    counts,
    cost,
    lower,
    upper,
    rhs,
    primal_start,
    dual_start,
    step_start,
):
    slots, tile, _ = tiles.shape
    row_blocks = rhs.shape[0] // tile
    col_blocks = cost.shape[0] // tile
    own = col_blocks // n_row
    phases = RUIZ + ITERS
    hbm = pl.BlockSpec(memory_space=pltpu.HBM)
    smem = pl.BlockSpec(memory_space=pltpu.SMEM)
    vmem = pl.BlockSpec(memory_space=pltpu.VMEM)
    f32 = jnp.float32

    def cols(x):
        return x.reshape(col_blocks, tile)

    def rows(x):
        return x.reshape(row_blocks, tile)

    dma = pltpu.SemaphoreType.DMA
    primal, dual, row_scale, col_scale, step = pl.pallas_call(
        functools.partial(kernel, n_row, n_col),
        out_shape=(
            jax.ShapeDtypeStruct((col_blocks, tile), f32),
            jax.ShapeDtypeStruct((row_blocks, tile), f32),
            jax.ShapeDtypeStruct((row_blocks, tile), f32),
            jax.ShapeDtypeStruct((col_blocks, tile), f32),
            jax.ShapeDtypeStruct((1, 1), f32),
        ),
        in_specs=[smem] * 2 + [hbm] * 9,
        out_specs=(vmem,) * 5,
        scratch_shapes=[
            pltpu.SMEM((slots,), jnp.int32),
            pltpu.SMEM((slots,), jnp.int32),
            pltpu.VMEM((slots, tile, tile), f32),
            pltpu.VMEM((col_blocks, tile), f32),
            pltpu.VMEM((col_blocks, tile), f32),
            pltpu.VMEM((col_blocks, tile), f32),
            pltpu.VMEM((row_blocks, tile), f32),
            pltpu.VMEM((col_blocks, tile), f32),
            pltpu.VMEM((row_blocks, tile), f32),
            dma((8,)),
            dma((slots,)),
            pltpu.VMEM((2, 8, tile), jnp.int32),
            pltpu.SMEM((2, 8, tile), jnp.int32),
            dma((2,)),
            pltpu.VMEM((2, tile, tile), jnp.int32),
            pltpu.VMEM((slots + 1, tile, tile), f32),
            pltpu.VMEM((row_blocks, tile, tile), f32),
            pltpu.VMEM((col_blocks, tile), f32),
            pltpu.VMEM((slots, tile), f32),
            pltpu.VMEM((phases, n_row, own + SIDE, tile), f32),
            pltpu.VMEM((phases, n_row, own + SIDE, tile), f32),
            pltpu.VMEM((phases, n_row, own + SIDE, tile), f32),
            pltpu.VMEM((phases + 1, n_col, row_blocks + SIDE, tile), f32),
            pltpu.VMEM((n_row, SIDE, tile), f32),
            dma((phases, n_row)),
            dma((phases, n_row)),
            dma((phases, n_row)),
            dma((phases, n_row)),
            dma((phases + 1, n_col)),
            dma((phases + 1, n_col)),
            dma((n_row,)),
            dma((n_row,)),
        ],
        compiler_params=pltpu.CompilerParams(
            collective_id=0, has_side_effects=True, vmem_limit_bytes=63 * 1024 * 1024
        ),
        name="equilibrate_and_iterate",
    )(
        counts,
        step_start,
        tile_rows,
        tile_cols,
        tiles,
        cols(cost),
        cols(lower),
        cols(upper),
        rows(rhs),
        cols(primal_start),
        rows(dual_start),
    )
    return (
        primal.reshape(-1),
        dual.reshape(-1),
        row_scale.reshape(-1),
        col_scale.reshape(-1),
        step.reshape(-1),
    )


def solution(mesh):
    in_specs = (
        P(("grp", "row", "col"), None, None),
        P(("grp", "row", "col")),
        P(("grp", "row", "col")),
        P(("grp", "row", "col")),
        P(("grp", "col")),
        P(("grp", "col")),
        P(("grp", "col")),
        P(("grp", "row")),
        P(("grp", "col")),
        P(("grp", "row")),
        P("grp"),
    )
    out_specs = (
        P(("grp", "col")),
        P(("grp", "row")),
        P(("grp", "row")),
        P(("grp", "col")),
        P("grp"),
    )
    local = functools.partial(body, mesh.shape["row"], mesh.shape["col"])
    return jax.shard_map(local, mesh=mesh, in_specs=in_specs, out_specs=out_specs, check_vma=False)
```

```python
import functools

import jax
import jax.numpy as jnp
from jax import lax
from jax.experimental import pallas as pl
from jax.experimental.pallas import tpu as pltpu
from jax.sharding import PartitionSpec as P

RUIZ = 4
ITERS = 2
EPS = 1e-06
MESH = pl.DeviceIdType.MESH
SIDE = 8


def kernel(
    n_row,
    n_col,
    count_ref,
    step_ref,
    tr_hbm,
    tc_hbm,
    tiles_hbm,
    cost_hbm,
    lower_hbm,
    upper_hbm,
    rhs_hbm,
    primal_hbm,
    dual_hbm,
    primal_out,
    dual_out,
    rscale_out,
    cscale_out,
    step_out,
    tr_ref,
    tc_ref,
    tiles_ref,
    cost_ref,
    lower_ref,
    upper_ref,
    rhs_ref,
    primal_ref,
    dual_ref,
    load_sem,
    tile_sem,
    listed,
    order,
    order_sem,
    keycol,
    running,
    rowmat,
    colvec,
    colpart,
    rs_send,
    rs_recv,
    ag_recv,
    pair_recv,
    last_recv,
    rs_ssem,
    rs_rsem,
    ag_ssem,
    ag_rsem,
    pair_ssem,
    pair_rsem,
    last_ssem,
    last_rsem,
):
    slots, tile, _ = tiles_ref.shape
    row_blocks = rhs_ref.shape[0]
    col_blocks = cost_ref.shape[0]
    own = col_blocks // n_row
    unroll = next(u for u in (8, 4, 2, 1) if slots % u == 0)
    grp = lax.axis_index("grp")
    me = lax.axis_index("row")
    core = lax.axis_index("col")
    mine = pl.ds(pl.multiple_of(me * own, own), own)
    count = count_ref[0]

    small = [
        pltpu.make_async_copy(source, target, load_sem.at[i])
        for i, (source, target) in enumerate(
            [
                (tr_hbm, tr_ref),
                (tc_hbm, tc_ref),
                (cost_hbm, cost_ref),
                (lower_hbm, lower_ref),
                (upper_hbm, upper_ref),
                (rhs_hbm, rhs_ref),
                (primal_hbm, primal_ref),
                (dual_hbm, dual_ref),
            ]
        )
    ]

    def tile_copy(i):
        some = pl.ds(i * unroll, unroll)
        return pltpu.make_async_copy(tiles_hbm.at[some], tiles_ref.at[some], tile_sem.at[i])

    def load_tiles(i, _):
        tile_copy(i).start()
        return 0

    small[0].start()
    small[1].start()
    lax.fori_loop(0, slots // unroll, load_tiles, 0)
    for copy in small[2:]:
        copy.start()

    barrier = pltpu.get_barrier_semaphore()

    def greet(step, _):
        peer = lax.rem(me + step, n_row)
        pl.semaphore_signal(barrier, inc=1, device_id=(grp, peer, core), device_id_type=MESH)
        return 0

    lax.fori_loop(1, n_row, greet, 0)
    for step in range(1, n_col):
        peer = lax.rem(core + step, n_col)
        pl.semaphore_signal(barrier, inc=1, device_id=(grp, me, peer), device_id_type=MESH)

    def over_peers(act):
        def body(step, _):
            act(lax.rem(me + step, n_row))
            return 0

        lax.fori_loop(1, n_row, body, 0)

    def length(k):
        return own if k < RUIZ else own + SIDE

    def rs_copy(k, peer, source):
        return pltpu.make_async_remote_copy(
            src_ref=rs_send.at[k, peer, pl.ds(0, length(k))],
            dst_ref=rs_recv.at[k, source, pl.ds(0, length(k))],
            send_sem=rs_ssem.at[k, peer],
            recv_sem=rs_rsem.at[k, source],
            device_id=(grp, peer, core),
            device_id_type=MESH,
        )

    def ag_copy(k, peer, source):
        return pltpu.make_async_remote_copy(
            src_ref=ag_recv.at[k, source, pl.ds(0, length(k))],
            dst_ref=ag_recv.at[k, source, pl.ds(0, length(k))],
            send_sem=ag_ssem.at[k, peer],
            recv_sem=ag_rsem.at[k, source],
            device_id=(grp, peer, core),
            device_id_type=MESH,
        )

    def last_copy(peer, source):
        return pltpu.make_async_remote_copy(
            src_ref=last_recv.at[source],
            dst_ref=last_recv.at[source],
            send_sem=last_ssem.at[peer],
            recv_sem=last_rsem.at[source],
            device_id=(grp, peer, core),
            device_id_type=MESH,
        )

    def pair_copy(k, peer, source):
        return pltpu.make_async_remote_copy(
            src_ref=pair_recv.at[k, source],
            dst_ref=pair_recv.at[k, source],
            send_sem=pair_ssem.at[k, peer],
            recv_sem=pair_rsem.at[k, source],
            device_id=(grp, me, peer),
            device_id_type=MESH,
        )

    def send_pair(k, value, side):
        pair_recv[k, core, 0:row_blocks] = value
        pair_recv[k, core, row_blocks : row_blocks + SIDE] = jnp.broadcast_to(side, (SIDE, tile))
        for step in range(1, n_col):
            pair_copy(k, lax.rem(core + step, n_col), core).start()

    def take_pair(k, combine):
        for step in range(1, n_col):
            peer = lax.rem(core + step, n_col)
            pair_copy(k, peer, peer).wait_recv()
        value = pair_recv[k, 0, 0:row_blocks]
        side = pair_recv[k, 0, row_blocks : row_blocks + SIDE]
        for c in range(1, n_col):
            value = combine(value, pair_recv[k, c, 0:row_blocks])
            side = side + pair_recv[k, c, row_blocks : row_blocks + SIDE]
        return value, side

    def scatter_cols(k, combine, side):
        owners = next(p for p in (4, 2, 1) if n_row % p == 0)
        ids = lax.broadcasted_iota(jnp.int32, (owners * own, tile), 0)

        groups = n_row // owners

        def some(i, _):
            p = lax.rem(me // owners + 1 + i, groups)
            first = p * (owners * own)

            def group(i, total):
                for u in range(unroll):
                    s = i * unroll + u
                    at = jnp.where(s < count, tc_ref[s] - first, -1)
                    part = colpart[pl.ds(s, 1), :]
                    total = combine(total, jnp.where(ids == at, part, 0.0))
                return total

            total = lax.fori_loop(
                0, slots // unroll, group, jnp.zeros((owners * own, tile), jnp.float32)
            )
            for q in range(owners):
                rs_send[k, p * owners + q, 0:own] = total[q * own : (q + 1) * own]
                if k >= RUIZ:
                    rs_send[k, p * owners + q, own : own + SIDE] = jnp.broadcast_to(
                        side, (SIDE, tile)
                    )
            for q in range(owners):
                owner = p * owners + q

                @pl.when(owner != me)
                def _():
                    rs_copy(k, owner, me).start()

            return 0

        lax.fori_loop(0, groups, some, 0)
        rs_recv[k, me, 0 : length(k)] = rs_send[k, me, 0 : length(k)]

    def take_rs(k, combine):
        over_peers(lambda peer: rs_copy(k, peer, peer).wait_recv())
        value = rs_recv[k, 0, 0:own]
        for p in range(1, n_row):
            value = combine(value, rs_recv[k, p, 0:own])
        if k < RUIZ:
            return value, None
        side = rs_recv[k, 0, own : own + SIDE]
        for p in range(1, n_row):
            side = side + rs_recv[k, p, own : own + SIDE]
        return value, side

    def send_ag(k, value, side):
        ag_recv[k, me, 0:own] = value
        if k >= RUIZ:
            ag_recv[k, me, own : own + SIDE] = jnp.broadcast_to(side, (SIDE, tile))
        over_peers(lambda peer: ag_copy(k, peer, me).start())

    def take_ag(k):
        over_peers(lambda peer: ag_copy(k, peer, peer).wait_recv())
        for p in range(n_row):
            colvec[p * own : (p + 1) * own, :] = ag_recv[k, p, 0:own]
        if k < RUIZ:
            return None
        side = ag_recv[k, 0, own : own + SIDE]
        for p in range(1, n_row):
            side = side + ag_recv[k, p, own : own + SIDE]
        return side

    def set_rows(vector):
        for r in range(row_blocks):
            wide = jnp.broadcast_to(vector[r : r + 1, :], (tile, tile))
            rowmat[r] = jnp.transpose(wide)

    def sort_slots():
        subs = lax.broadcasted_iota(jnp.int32, (tile, tile), 0)
        lanes = lax.broadcasted_iota(jnp.int32, (tile, tile), 1)
        lane = lax.broadcasted_iota(jnp.int32, (1, tile), 1)
        far = row_blocks + 1
        keycol[0] = jnp.full((tile, tile), far, jnp.int32)
        keys = jnp.full((1, tile), far, jnp.int32)
        for s in range(slots):
            key = jnp.where(s < count, tr_ref[s], row_blocks)
            keycol[0, s : s + 1, :] = jnp.full((1, tile), key, jnp.int32)
            keys = jnp.where(lane == s, key, keys)
        col = keycol[0]
        ahead = (col < keys) | ((col == keys) & (subs < lanes))
        listed[0, 0:1, :] = jnp.sum(ahead.astype(jnp.int32), axis=0, keepdims=True)
        copy = pltpu.make_async_copy(listed.at[0], order.at[0], order_sem.at[0])
        copy.start()
        until = jnp.sum((col <= lanes).astype(jnp.int32), axis=0, keepdims=True)
        held = jnp.sum((col == lanes).astype(jnp.int32), axis=0, keepdims=True)
        listed[1, 2:3, :] = jnp.where(held > 0, until - 1, slots)
        copy.wait()
        keycol[1] = jnp.full((tile, tile), 2 * tile, jnp.int32)
        for s in range(slots):
            keycol[1, s : s + 1, :] = jnp.full((1, tile), order[0, 0, s], jnp.int32)
        rank = keycol[1]
        here = jnp.sum(jnp.where(rank == lanes, col, 0), axis=0, keepdims=True)
        left = jnp.sum(jnp.where(rank == lanes - 1, col, 0), axis=0, keepdims=True)
        listed[1, 0:1, :] = jnp.sum(jnp.where(rank == lanes, subs, 0), axis=0, keepdims=True)
        listed[1, 1:2, :] = ((here == left) & (lane > 0)).astype(jnp.int32)
        copy = pltpu.make_async_copy(listed.at[1], order.at[1], order_sem.at[1])
        copy.start()
        running[slots] = jnp.zeros((tile, tile), jnp.float32)
        copy.wait()

    def col_pass(reduce, transform, first=False):
        def group(i, _):
            if first:
                tile_copy(i).wait()
            for u in range(unroll):
                s = i * unroll + u
                block = tiles_ref[s] if first else tiles_ref[s] * rowmat[tr_ref[s]]
                colpart[pl.ds(s, 1), :] = reduce(transform(block), axis=0, keepdims=True)
            return 0

        lax.fori_loop(0, slots // unroll, group, 0)

    def row_pass(reduce, transform, combine, first=False):
        def group(i, total):
            for u in range(unroll):
                j = i * unroll + u
                s = order[1, 0, j]
                block = tiles_ref[s]
                if not first:
                    block = block * colvec[pl.ds(tc_ref[s], 1), :]
                total = jnp.where(order[1, 1, j] == 1, total, 0.0)
                total = combine(total, transform(block))
                running[j] = total
            return total

        lax.fori_loop(0, slots // unroll, group, jnp.zeros((tile, tile), jnp.float32))
        lanes = lax.broadcasted_iota(jnp.int32, (tile, tile), 1)
        total = jnp.zeros((tile, tile), jnp.float32)
        for r in range(row_blocks):
            part = reduce(running[order[1, 2, r]], axis=1, keepdims=True)
            total = jnp.where(lanes == r, part, total)
        return jnp.transpose(total)[0:row_blocks]

    def plain(block):
        return block

    add = jnp.add
    none = jnp.zeros((1, tile), jnp.float32)

    def total_of(value):
        part = jnp.sum(jnp.sum(value, axis=0, keepdims=True), axis=1, keepdims=True)
        return jnp.broadcast_to(part, (1, tile))

    row_scale = jnp.ones((row_blocks, tile), jnp.float32)
    col_scale = jnp.ones((own, tile), jnp.float32)
    small[0].wait()
    small[1].wait()
    for sweep in range(RUIZ):
        if sweep > 0:
            set_rows(row_scale)
        col_pass(jnp.max, jnp.abs, sweep == 0)
        if sweep == 0:
            pl.semaphore_wait(barrier, n_row + n_col - 2)
        scatter_cols(sweep, jnp.maximum, none)
        if sweep == 0:
            sort_slots()
        else:
            take_ag(sweep - 1)
        row_local = row_pass(jnp.max, jnp.abs, jnp.maximum, sweep == 0)
        send_pair(sweep, row_local, none)
        col_peak = take_rs(sweep, jnp.maximum)[0] * col_scale
        col_scale = col_scale / jnp.sqrt(col_peak + EPS)
        send_ag(sweep, col_scale, none)
        row_peak = take_pair(sweep, jnp.maximum)[0] * row_scale
        row_scale = row_scale / jnp.sqrt(row_peak + EPS)

    for copy in small[2:]:
        copy.wait()
    rscale_out[...] = row_scale
    rhs_scaled = row_scale * rhs_ref[...]
    dual = dual_ref[...] / row_scale
    set_rows(row_scale * dual)
    col_pass(jnp.sum, plain)
    scatter_cols(RUIZ, add, total_of(rhs_scaled * rhs_scaled))

    take_ag(RUIZ - 1)
    whole_scale = colvec[...]
    cscale_out[...] = whole_scale
    whole_cost = whole_scale * cost_ref[...]
    colvec[...] = whole_scale * (primal_ref[...] / whole_scale)
    send_pair(RUIZ, row_pass(jnp.sum, plain, add), total_of(whole_cost * whole_cost))

    cost_scaled = col_scale * cost_ref[mine, :]
    lower_scaled = lower_ref[mine, :] / col_scale
    upper_scaled = upper_ref[mine, :] / col_scale
    primal = primal_ref[mine, :] / col_scale
    eta = jnp.full((1, tile), step_ref[0], jnp.float32)

    side_rows = lax.broadcasted_iota(jnp.int32, (SIDE, tile), 0)
    weight = None
    image = None
    before = None
    for k in range(ITERS):
        gradient, side = take_rs(RUIZ + k, add)
        gradient = col_scale * gradient
        if k == 0:
            image, cost_side = take_pair(RUIZ, add)
            image = row_scale * image
            weight = jnp.sqrt(cost_side[0:1] + EPS) / jnp.sqrt(side[0:1] + EPS)
        else:
            eta = next_step(k - 1, eta, weight, before, side)
        primal_next = jnp.clip(
            primal - eta / weight * (cost_scaled - gradient), lower_scaled, upper_scaled
        )
        moved = primal_next - primal
        send_ag(RUIZ + k, col_scale * primal_next, total_of(moved * moved))
        primal = primal_next
        moved_sq = take_ag(RUIZ + k)[0:1]
        send_pair(RUIZ + 1 + k, row_pass(jnp.sum, plain, add), moved_sq)
        image_next, before = take_pair(RUIZ + 1 + k, add)
        before = before[0:1]
        image_next = row_scale * image_next
        dual_next = jnp.maximum(
            dual + eta * weight * (rhs_scaled - 2.0 * image_next + image), 0.0
        )
        moved = dual_next - dual
        both = jnp.where(
            side_rows == 0,
            total_of(moved * moved),
            total_of(moved * (image_next - image)),
        )
        dual, image = dual_next, image_next
        if k < ITERS - 1:
            set_rows(row_scale * dual)
            col_pass(jnp.sum, plain)
            scatter_cols(RUIZ + 1 + k, add, both)
        else:
            last_recv[me] = both
            over_peers(lambda peer: last_copy(peer, me).start())
            primal_out[...] = colvec[...]
            dual_out[...] = row_scale * dual
            over_peers(lambda peer: last_copy(peer, peer).wait_recv())
            side = last_recv[0]
            for p in range(1, n_row):
                side = side + last_recv[p]
            eta = next_step(k, eta, weight, before, side)
    step_out[...] = eta[:, 0:1]

    for k in range(RUIZ + ITERS):
        over_peers(lambda peer: rs_copy(k, peer, me).wait_send())
        over_peers(lambda peer: ag_copy(k, peer, me).wait_send())
    for k in range(RUIZ + ITERS + 1):
        for step in range(1, n_col):
            pair_copy(k, lax.rem(core + step, n_col), core).wait_send()
    over_peers(lambda peer: last_copy(peer, me).wait_send())


def deliver(*refs):
    sources, targets, sem = refs[:4], refs[4:8], refs[8]
    copies = [
        pltpu.make_async_copy(source, target, sem.at[i])
        for i, (source, target) in enumerate(zip(sources, targets))
    ]
    for copy in copies:
        copy.start()
    for copy in copies:
        copy.wait()


def next_step(k, eta, weight, primal_sq, side):
    dual_sq, coupling = side[0:1], side[1:2]
    movement = 0.5 * weight * primal_sq + 0.5 / weight * dual_sq + EPS
    growth = (1.0 + (k + 2.0) ** (-0.6)) * eta
    limit = (1.0 - (k + 2.0) ** (-0.3)) * movement
    return limit / jnp.maximum(jnp.abs(coupling), limit / growth)


def body(
    n_row,
    n_col,
    tiles,
    tile_rows,
    tile_cols,
    counts,
    cost,
    lower,
    upper,
    rhs,
    primal_start,
    dual_start,
    step_start,
):
    slots, tile, _ = tiles.shape
    row_blocks = rhs.shape[0] // tile
    col_blocks = cost.shape[0] // tile
    own = col_blocks // n_row
    phases = RUIZ + ITERS
    hbm = pl.BlockSpec(memory_space=pltpu.HBM)
    smem = pl.BlockSpec(memory_space=pltpu.SMEM)
    vmem = pl.BlockSpec(memory_space=pltpu.VMEM)
    f32 = jnp.float32

    def cols(x):
        return x.reshape(col_blocks, tile)

    def rows(x):
        return x.reshape(row_blocks, tile)

    dma = pltpu.SemaphoreType.DMA
    primal, dual, row_scale, col_scale, step = pl.pallas_call(
        functools.partial(kernel, n_row, n_col),
        out_shape=(
            jax.ShapeDtypeStruct((col_blocks, tile), f32),
            jax.ShapeDtypeStruct((row_blocks, tile), f32),
            jax.ShapeDtypeStruct((row_blocks, tile), f32),
            jax.ShapeDtypeStruct((col_blocks, tile), f32),
            jax.ShapeDtypeStruct((1, 1), f32),
        ),
        in_specs=[smem] * 2 + [hbm] * 9,
        out_specs=(vmem,) * 5,
        scratch_shapes=[
            pltpu.SMEM((slots,), jnp.int32),
            pltpu.SMEM((slots,), jnp.int32),
            pltpu.VMEM((slots, tile, tile), f32),
            pltpu.VMEM((col_blocks, tile), f32),
            pltpu.VMEM((col_blocks, tile), f32),
            pltpu.VMEM((col_blocks, tile), f32),
            pltpu.VMEM((row_blocks, tile), f32),
            pltpu.VMEM((col_blocks, tile), f32),
            pltpu.VMEM((row_blocks, tile), f32),
            dma((8,)),
            dma((slots,)),
            pltpu.VMEM((2, 8, tile), jnp.int32),
            pltpu.SMEM((2, 8, tile), jnp.int32),
            dma((2,)),
            pltpu.VMEM((2, tile, tile), jnp.int32),
            pltpu.VMEM((slots + 1, tile, tile), f32),
            pltpu.VMEM((row_blocks, tile, tile), f32),
            pltpu.VMEM((col_blocks, tile), f32),
            pltpu.VMEM((slots, tile), f32),
            pltpu.VMEM((phases, n_row, own + SIDE, tile), f32),
            pltpu.VMEM((phases, n_row, own + SIDE, tile), f32),
            pltpu.VMEM((phases, n_row, own + SIDE, tile), f32),
            pltpu.VMEM((phases + 1, n_col, row_blocks + SIDE, tile), f32),
            pltpu.VMEM((n_row, SIDE, tile), f32),
            dma((phases, n_row)),
            dma((phases, n_row)),
            dma((phases, n_row)),
            dma((phases, n_row)),
            dma((phases + 1, n_col)),
            dma((phases + 1, n_col)),
            dma((n_row,)),
            dma((n_row,)),
        ],
        compiler_params=pltpu.CompilerParams(
            collective_id=0, has_side_effects=True, vmem_limit_bytes=63 * 1024 * 1024
        ),
        name="equilibrate_and_iterate",
    )(
        counts,
        step_start,
        tile_rows,
        tile_cols,
        tiles,
        cols(cost),
        cols(lower),
        cols(upper),
        rows(rhs),
        cols(primal_start),
        rows(dual_start),
    )
    results = (primal, dual, row_scale, col_scale)
    primal, dual, row_scale, col_scale = pl.pallas_call(
        deliver,
        out_shape=tuple(jax.ShapeDtypeStruct(x.shape, f32) for x in results),
        in_specs=[hbm] * 4,
        out_specs=(hbm,) * 4,
        scratch_shapes=[dma((4,))],
        compiler_params=pltpu.CompilerParams(vmem_limit_bytes=63 * 1024 * 1024),
        name="deliver",
    )(*results)
    return (
        primal.reshape(-1),
        dual.reshape(-1),
        row_scale.reshape(-1),
        col_scale.reshape(-1),
        step.reshape(-1),
    )


def solution(mesh):
    in_specs = (
        P(("grp", "row", "col"), None, None),
        P(("grp", "row", "col")),
        P(("grp", "row", "col")),
        P(("grp", "row", "col")),
        P(("grp", "col")),
        P(("grp", "col")),
        P(("grp", "col")),
        P(("grp", "row")),
        P(("grp", "col")),
        P(("grp", "row")),
        P("grp"),
    )
    out_specs = (
        P(("grp", "col")),
        P(("grp", "row")),
        P(("grp", "row")),
        P(("grp", "col")),
        P("grp"),
    )
    local = functools.partial(body, mesh.shape["row"], mesh.shape["col"])
    return jax.shard_map(local, mesh=mesh, in_specs=in_specs, out_specs=out_specs, check_vma=False)
```

```python
import functools

import jax
import jax.numpy as jnp
from jax import lax
from jax.experimental import pallas as pl
from jax.experimental.pallas import tpu as pltpu
from jax.sharding import PartitionSpec as P

RUIZ = 4
ITERS = 2
EPS = 1e-06
MESH = pl.DeviceIdType.MESH
SIDE = 8


def kernel(
    n_row,
    n_col,
    count_ref,
    step_ref,
    tr_hbm,
    tc_hbm,
    tiles_hbm,
    cost_hbm,
    lower_hbm,
    upper_hbm,
    rhs_hbm,
    primal_hbm,
    dual_hbm,
    primal_to,
    dual_to,
    rscale_to,
    cscale_to,
    step_out,
    tr_ref,
    tc_ref,
    tiles_ref,
    cost_ref,
    lower_ref,
    upper_ref,
    rhs_ref,
    primal_ref,
    dual_ref,
    load_sem,
    tile_sem,
    listed,
    order,
    order_sem,
    keycol,
    running,
    rowmat,
    colvec,
    colpart,
    rs_send,
    rs_recv,
    ag_recv,
    pair_recv,
    last_recv,
    rs_ssem,
    rs_rsem,
    ag_ssem,
    ag_rsem,
    pair_ssem,
    pair_rsem,
    last_ssem,
    last_rsem,
    primal_out,
    dual_out,
    rscale_out,
    cscale_out,
    out_sem,
):
    slots, tile, _ = tiles_ref.shape
    row_blocks = rhs_ref.shape[0]
    col_blocks = cost_ref.shape[0]
    own = col_blocks // n_row
    unroll = next(u for u in (8, 4, 2, 1) if slots % u == 0)
    grp = lax.axis_index("grp")
    me = lax.axis_index("row")
    core = lax.axis_index("col")
    mine = pl.ds(pl.multiple_of(me * own, own), own)
    count = count_ref[0]

    small = [
        pltpu.make_async_copy(source, target, load_sem.at[i])
        for i, (source, target) in enumerate(
            [
                (tr_hbm, tr_ref),
                (tc_hbm, tc_ref),
                (cost_hbm, cost_ref),
                (lower_hbm, lower_ref),
                (upper_hbm, upper_ref),
                (rhs_hbm, rhs_ref),
                (primal_hbm, primal_ref),
                (dual_hbm, dual_ref),
            ]
        )
    ]

    outward = [
        pltpu.make_async_copy(source, target, out_sem.at[i])
        for i, (source, target) in enumerate(
            [
                (primal_out, primal_to),
                (dual_out, dual_to),
                (rscale_out, rscale_to),
                (cscale_out, cscale_to),
            ]
        )
    ]

    def tile_copy(i):
        some = pl.ds(i * unroll, unroll)
        return pltpu.make_async_copy(tiles_hbm.at[some], tiles_ref.at[some], tile_sem.at[i])

    def load_tiles(i, _):
        tile_copy(i).start()
        return 0

    small[0].start()
    small[1].start()
    lax.fori_loop(0, slots // unroll, load_tiles, 0)
    for copy in small[2:]:
        copy.start()

    barrier = pltpu.get_barrier_semaphore()

    def greet(step, _):
        peer = lax.rem(me + step, n_row)
        pl.semaphore_signal(barrier, inc=1, device_id=(grp, peer, core), device_id_type=MESH)
        return 0

    lax.fori_loop(1, n_row, greet, 0)
    for step in range(1, n_col):
        peer = lax.rem(core + step, n_col)
        pl.semaphore_signal(barrier, inc=1, device_id=(grp, me, peer), device_id_type=MESH)

    def over_peers(act):
        def body(step, _):
            act(lax.rem(me + step, n_row))
            return 0

        lax.fori_loop(1, n_row, body, 0)

    def length(k):
        return own if k < RUIZ else own + SIDE

    def rs_copy(k, peer, source):
        return pltpu.make_async_remote_copy(
            src_ref=rs_send.at[k, peer, pl.ds(0, length(k))],
            dst_ref=rs_recv.at[k, source, pl.ds(0, length(k))],
            send_sem=rs_ssem.at[k, peer],
            recv_sem=rs_rsem.at[k, source],
            device_id=(grp, peer, core),
            device_id_type=MESH,
        )

    def ag_copy(k, peer, source):
        return pltpu.make_async_remote_copy(
            src_ref=ag_recv.at[k, source, pl.ds(0, length(k))],
            dst_ref=ag_recv.at[k, source, pl.ds(0, length(k))],
            send_sem=ag_ssem.at[k, peer],
            recv_sem=ag_rsem.at[k, source],
            device_id=(grp, peer, core),
            device_id_type=MESH,
        )

    def last_copy(peer, source):
        return pltpu.make_async_remote_copy(
            src_ref=last_recv.at[source],
            dst_ref=last_recv.at[source],
            send_sem=last_ssem.at[peer],
            recv_sem=last_rsem.at[source],
            device_id=(grp, peer, core),
            device_id_type=MESH,
        )

    def pair_copy(k, peer, source):
        return pltpu.make_async_remote_copy(
            src_ref=pair_recv.at[k, source],
            dst_ref=pair_recv.at[k, source],
            send_sem=pair_ssem.at[k, peer],
            recv_sem=pair_rsem.at[k, source],
            device_id=(grp, me, peer),
            device_id_type=MESH,
        )

    def send_pair(k, value, side):
        pair_recv[k, core, 0:row_blocks] = value
        pair_recv[k, core, row_blocks : row_blocks + SIDE] = jnp.broadcast_to(side, (SIDE, tile))
        for step in range(1, n_col):
            pair_copy(k, lax.rem(core + step, n_col), core).start()

    def take_pair(k, combine):
        for step in range(1, n_col):
            peer = lax.rem(core + step, n_col)
            pair_copy(k, peer, peer).wait_recv()
        value = pair_recv[k, 0, 0:row_blocks]
        side = pair_recv[k, 0, row_blocks : row_blocks + SIDE]
        for c in range(1, n_col):
            value = combine(value, pair_recv[k, c, 0:row_blocks])
            side = side + pair_recv[k, c, row_blocks : row_blocks + SIDE]
        return value, side

    def scatter_cols(k, combine, side):
        owners = next(p for p in (4, 2, 1) if n_row % p == 0)
        ids = lax.broadcasted_iota(jnp.int32, (owners * own, tile), 0)

        groups = n_row // owners

        def some(i, _):
            p = lax.rem(me // owners + 1 + i, groups)
            first = p * (owners * own)

            def group(i, total):
                for u in range(unroll):
                    s = i * unroll + u
                    at = jnp.where(s < count, tc_ref[s] - first, -1)
                    part = colpart[pl.ds(s, 1), :]
                    total = combine(total, jnp.where(ids == at, part, 0.0))
                return total

            total = lax.fori_loop(
                0, slots // unroll, group, jnp.zeros((owners * own, tile), jnp.float32)
            )
            for q in range(owners):
                rs_send[k, p * owners + q, 0:own] = total[q * own : (q + 1) * own]
                if k >= RUIZ:
                    rs_send[k, p * owners + q, own : own + SIDE] = jnp.broadcast_to(
                        side, (SIDE, tile)
                    )
            for q in range(owners):
                owner = p * owners + q

                @pl.when(owner != me)
                def _():
                    rs_copy(k, owner, me).start()

            return 0

        lax.fori_loop(0, groups, some, 0)
        rs_recv[k, me, 0 : length(k)] = rs_send[k, me, 0 : length(k)]

    def take_rs(k, combine):
        over_peers(lambda peer: rs_copy(k, peer, peer).wait_recv())
        value = rs_recv[k, 0, 0:own]
        for p in range(1, n_row):
            value = combine(value, rs_recv[k, p, 0:own])
        if k < RUIZ:
            return value, None
        side = rs_recv[k, 0, own : own + SIDE]
        for p in range(1, n_row):
            side = side + rs_recv[k, p, own : own + SIDE]
        return value, side

    def send_ag(k, value, side):
        ag_recv[k, me, 0:own] = value
        if k >= RUIZ:
            ag_recv[k, me, own : own + SIDE] = jnp.broadcast_to(side, (SIDE, tile))
        over_peers(lambda peer: ag_copy(k, peer, me).start())

    def take_ag(k):
        over_peers(lambda peer: ag_copy(k, peer, peer).wait_recv())
        for p in range(n_row):
            colvec[p * own : (p + 1) * own, :] = ag_recv[k, p, 0:own]
        if k < RUIZ:
            return None
        side = ag_recv[k, 0, own : own + SIDE]
        for p in range(1, n_row):
            side = side + ag_recv[k, p, own : own + SIDE]
        return side

    def set_rows(vector):
        for r in range(row_blocks):
            wide = jnp.broadcast_to(vector[r : r + 1, :], (tile, tile))
            rowmat[r] = jnp.transpose(wide)

    def sort_slots():
        subs = lax.broadcasted_iota(jnp.int32, (tile, tile), 0)
        lanes = lax.broadcasted_iota(jnp.int32, (tile, tile), 1)
        lane = lax.broadcasted_iota(jnp.int32, (1, tile), 1)
        far = row_blocks + 1
        keycol[0] = jnp.full((tile, tile), far, jnp.int32)
        keys = jnp.full((1, tile), far, jnp.int32)
        for s in range(slots):
            key = jnp.where(s < count, tr_ref[s], row_blocks)
            keycol[0, s : s + 1, :] = jnp.full((1, tile), key, jnp.int32)
            keys = jnp.where(lane == s, key, keys)
        col = keycol[0]
        ahead = (col < keys) | ((col == keys) & (subs < lanes))
        listed[0, 0:1, :] = jnp.sum(ahead.astype(jnp.int32), axis=0, keepdims=True)
        copy = pltpu.make_async_copy(listed.at[0], order.at[0], order_sem.at[0])
        copy.start()
        until = jnp.sum((col <= lanes).astype(jnp.int32), axis=0, keepdims=True)
        held = jnp.sum((col == lanes).astype(jnp.int32), axis=0, keepdims=True)
        listed[1, 2:3, :] = jnp.where(held > 0, until - 1, slots)
        copy.wait()
        keycol[1] = jnp.full((tile, tile), 2 * tile, jnp.int32)
        for s in range(slots):
            keycol[1, s : s + 1, :] = jnp.full((1, tile), order[0, 0, s], jnp.int32)
        rank = keycol[1]
        here = jnp.sum(jnp.where(rank == lanes, col, 0), axis=0, keepdims=True)
        left = jnp.sum(jnp.where(rank == lanes - 1, col, 0), axis=0, keepdims=True)
        listed[1, 0:1, :] = jnp.sum(jnp.where(rank == lanes, subs, 0), axis=0, keepdims=True)
        listed[1, 1:2, :] = ((here == left) & (lane > 0)).astype(jnp.int32)
        copy = pltpu.make_async_copy(listed.at[1], order.at[1], order_sem.at[1])
        copy.start()
        running[slots] = jnp.zeros((tile, tile), jnp.float32)
        copy.wait()

    def col_pass(reduce, transform, first=False):
        def group(i, _):
            if first:
                tile_copy(i).wait()
            for u in range(unroll):
                s = i * unroll + u
                block = tiles_ref[s] if first else tiles_ref[s] * rowmat[tr_ref[s]]
                colpart[pl.ds(s, 1), :] = reduce(transform(block), axis=0, keepdims=True)
            return 0

        lax.fori_loop(0, slots // unroll, group, 0)

    def row_pass(reduce, transform, combine, first=False):
        def group(i, total):
            for u in range(unroll):
                j = i * unroll + u
                s = order[1, 0, j]
                block = tiles_ref[s]
                if not first:
                    block = block * colvec[pl.ds(tc_ref[s], 1), :]
                total = jnp.where(order[1, 1, j] == 1, total, 0.0)
                total = combine(total, transform(block))
                running[j] = total
            return total

        lax.fori_loop(0, slots // unroll, group, jnp.zeros((tile, tile), jnp.float32))
        lanes = lax.broadcasted_iota(jnp.int32, (tile, tile), 1)
        total = jnp.zeros((tile, tile), jnp.float32)
        for r in range(row_blocks):
            part = reduce(running[order[1, 2, r]], axis=1, keepdims=True)
            total = jnp.where(lanes == r, part, total)
        return jnp.transpose(total)[0:row_blocks]

    def plain(block):
        return block

    add = jnp.add
    none = jnp.zeros((1, tile), jnp.float32)

    def total_of(value):
        part = jnp.sum(jnp.sum(value, axis=0, keepdims=True), axis=1, keepdims=True)
        return jnp.broadcast_to(part, (1, tile))

    row_scale = jnp.ones((row_blocks, tile), jnp.float32)
    col_scale = jnp.ones((own, tile), jnp.float32)
    small[0].wait()
    small[1].wait()
    for sweep in range(RUIZ):
        if sweep > 0:
            set_rows(row_scale)
        col_pass(jnp.max, jnp.abs, sweep == 0)
        if sweep == 0:
            pl.semaphore_wait(barrier, n_row + n_col - 2)
        scatter_cols(sweep, jnp.maximum, none)
        if sweep == 0:
            sort_slots()
        else:
            take_ag(sweep - 1)
        row_local = row_pass(jnp.max, jnp.abs, jnp.maximum, sweep == 0)
        send_pair(sweep, row_local, none)
        col_peak = take_rs(sweep, jnp.maximum)[0] * col_scale
        col_scale = col_scale / jnp.sqrt(col_peak + EPS)
        send_ag(sweep, col_scale, none)
        row_peak = take_pair(sweep, jnp.maximum)[0] * row_scale
        row_scale = row_scale / jnp.sqrt(row_peak + EPS)

    for copy in small[2:]:
        copy.wait()
    rscale_out[...] = row_scale
    outward[2].start()
    rhs_scaled = row_scale * rhs_ref[...]
    dual = dual_ref[...] / row_scale
    set_rows(row_scale * dual)
    col_pass(jnp.sum, plain)
    scatter_cols(RUIZ, add, total_of(rhs_scaled * rhs_scaled))

    take_ag(RUIZ - 1)
    whole_scale = colvec[...]
    cscale_out[...] = whole_scale
    outward[3].start()
    whole_cost = whole_scale * cost_ref[...]
    colvec[...] = whole_scale * (primal_ref[...] / whole_scale)
    send_pair(RUIZ, row_pass(jnp.sum, plain, add), total_of(whole_cost * whole_cost))

    cost_scaled = col_scale * cost_ref[mine, :]
    lower_scaled = lower_ref[mine, :] / col_scale
    upper_scaled = upper_ref[mine, :] / col_scale
    primal = primal_ref[mine, :] / col_scale
    eta = jnp.full((1, tile), step_ref[0], jnp.float32)

    side_rows = lax.broadcasted_iota(jnp.int32, (SIDE, tile), 0)
    weight = None
    image = None
    before = None
    for k in range(ITERS):
        gradient, side = take_rs(RUIZ + k, add)
        gradient = col_scale * gradient
        if k == 0:
            image, cost_side = take_pair(RUIZ, add)
            image = row_scale * image
            weight = jnp.sqrt(cost_side[0:1] + EPS) / jnp.sqrt(side[0:1] + EPS)
        else:
            eta = next_step(k - 1, eta, weight, before, side)
        primal_next = jnp.clip(
            primal - eta / weight * (cost_scaled - gradient), lower_scaled, upper_scaled
        )
        moved = primal_next - primal
        send_ag(RUIZ + k, col_scale * primal_next, total_of(moved * moved))
        primal = primal_next
        moved_sq = take_ag(RUIZ + k)[0:1]
        send_pair(RUIZ + 1 + k, row_pass(jnp.sum, plain, add), moved_sq)
        image_next, before = take_pair(RUIZ + 1 + k, add)
        before = before[0:1]
        image_next = row_scale * image_next
        dual_next = jnp.maximum(
            dual + eta * weight * (rhs_scaled - 2.0 * image_next + image), 0.0
        )
        moved = dual_next - dual
        both = jnp.where(
            side_rows == 0,
            total_of(moved * moved),
            total_of(moved * (image_next - image)),
        )
        dual, image = dual_next, image_next
        if k < ITERS - 1:
            set_rows(row_scale * dual)
            col_pass(jnp.sum, plain)
            scatter_cols(RUIZ + 1 + k, add, both)
        else:
            last_recv[me] = both
            over_peers(lambda peer: last_copy(peer, me).start())
            primal_out[...] = colvec[...]
            outward[0].start()
            dual_out[...] = row_scale * dual
            outward[1].start()
            for m in range(RUIZ + ITERS):
                over_peers(lambda peer: rs_copy(m, peer, me).wait_send())
                over_peers(lambda peer: ag_copy(m, peer, me).wait_send())
            for m in range(RUIZ + ITERS + 1):
                for step in range(1, n_col):
                    pair_copy(m, lax.rem(core + step, n_col), core).wait_send()
            over_peers(lambda peer: last_copy(peer, peer).wait_recv())
            side = last_recv[0]
            for p in range(1, n_row):
                side = side + last_recv[p]
            eta = next_step(k, eta, weight, before, side)
    step_out[...] = eta[:, 0:1]

    over_peers(lambda peer: last_copy(peer, me).wait_send())
    for copy in outward:
        copy.wait()


def deliver(*refs):
    sources, targets, stages = refs[:4], refs[4:8], refs[8:12]
    in_sem, out_sem = refs[12:]
    inward = [pltpu.make_async_copy(sources[i], stages[i], in_sem.at[i]) for i in range(4)]
    outward = [pltpu.make_async_copy(stages[i], targets[i], out_sem.at[i]) for i in range(4)]
    for copy in inward:
        copy.start()
    for i in range(4):
        inward[i].wait()
        outward[i].start()
    for copy in outward:
        copy.wait()


def next_step(k, eta, weight, primal_sq, side):
    dual_sq, coupling = side[0:1], side[1:2]
    movement = 0.5 * weight * primal_sq + 0.5 / weight * dual_sq + EPS
    growth = (1.0 + (k + 2.0) ** (-0.6)) * eta
    limit = (1.0 - (k + 2.0) ** (-0.3)) * movement
    return limit / jnp.maximum(jnp.abs(coupling), limit / growth)


def body(
    n_row,
    n_col,
    tiles,
    tile_rows,
    tile_cols,
    counts,
    cost,
    lower,
    upper,
    rhs,
    primal_start,
    dual_start,
    step_start,
):
    slots, tile, _ = tiles.shape
    row_blocks = rhs.shape[0] // tile
    col_blocks = cost.shape[0] // tile
    own = col_blocks // n_row
    phases = RUIZ + ITERS
    hbm = pl.BlockSpec(memory_space=pltpu.HBM)
    smem = pl.BlockSpec(memory_space=pltpu.SMEM)
    vmem = pl.BlockSpec(memory_space=pltpu.VMEM)
    f32 = jnp.float32

    def cols(x):
        return x.reshape(col_blocks, tile)

    def rows(x):
        return x.reshape(row_blocks, tile)

    dma = pltpu.SemaphoreType.DMA
    primal, dual, row_scale, col_scale, step = pl.pallas_call(
        functools.partial(kernel, n_row, n_col),
        out_shape=(
            jax.ShapeDtypeStruct((col_blocks, tile), f32),
            jax.ShapeDtypeStruct((row_blocks, tile), f32),
            jax.ShapeDtypeStruct((row_blocks, tile), f32),
            jax.ShapeDtypeStruct((col_blocks, tile), f32),
            jax.ShapeDtypeStruct((1, 1), f32),
        ),
        in_specs=[smem] * 2 + [hbm] * 9,
        out_specs=(hbm,) * 4 + (vmem,),
        scratch_shapes=[
            pltpu.SMEM((slots,), jnp.int32),
            pltpu.SMEM((slots,), jnp.int32),
            pltpu.VMEM((slots, tile, tile), f32),
            pltpu.VMEM((col_blocks, tile), f32),
            pltpu.VMEM((col_blocks, tile), f32),
            pltpu.VMEM((col_blocks, tile), f32),
            pltpu.VMEM((row_blocks, tile), f32),
            pltpu.VMEM((col_blocks, tile), f32),
            pltpu.VMEM((row_blocks, tile), f32),
            dma((8,)),
            dma((slots,)),
            pltpu.VMEM((2, 8, tile), jnp.int32),
            pltpu.SMEM((2, 8, tile), jnp.int32),
            dma((2,)),
            pltpu.VMEM((2, tile, tile), jnp.int32),
            pltpu.VMEM((slots + 1, tile, tile), f32),
            pltpu.VMEM((row_blocks, tile, tile), f32),
            pltpu.VMEM((col_blocks, tile), f32),
            pltpu.VMEM((slots, tile), f32),
            pltpu.VMEM((phases, n_row, own + SIDE, tile), f32),
            pltpu.VMEM((phases, n_row, own + SIDE, tile), f32),
            pltpu.VMEM((phases, n_row, own + SIDE, tile), f32),
            pltpu.VMEM((phases + 1, n_col, row_blocks + SIDE, tile), f32),
            pltpu.VMEM((n_row, SIDE, tile), f32),
            dma((phases, n_row)),
            dma((phases, n_row)),
            dma((phases, n_row)),
            dma((phases, n_row)),
            dma((phases + 1, n_col)),
            dma((phases + 1, n_col)),
            dma((n_row,)),
            dma((n_row,)),
            pltpu.VMEM((col_blocks, tile), f32),
            pltpu.VMEM((row_blocks, tile), f32),
            pltpu.VMEM((row_blocks, tile), f32),
            pltpu.VMEM((col_blocks, tile), f32),
            dma((4,)),
        ],
        compiler_params=pltpu.CompilerParams(
            collective_id=0, has_side_effects=True, vmem_limit_bytes=63 * 1024 * 1024
        ),
        name="equilibrate_and_iterate",
    )(
        counts,
        step_start,
        tile_rows,
        tile_cols,
        tiles,
        cols(cost),
        cols(lower),
        cols(upper),
        rows(rhs),
        cols(primal_start),
        rows(dual_start),
    )
    results = (primal, dual, row_scale, col_scale)
    primal, dual, row_scale, col_scale = pl.pallas_call(
        deliver,
        out_shape=tuple(jax.ShapeDtypeStruct(x.shape, f32) for x in results),
        in_specs=[hbm] * 4,
        out_specs=(hbm,) * 4,
        scratch_shapes=[pltpu.VMEM(x.shape, f32) for x in results] + [dma((4,)), dma((4,))],
        compiler_params=pltpu.CompilerParams(vmem_limit_bytes=63 * 1024 * 1024),
        name="deliver",
    )(*results)
    return (
        primal.reshape(-1),
        dual.reshape(-1),
        row_scale.reshape(-1),
        col_scale.reshape(-1),
        step.reshape(-1),
    )


def solution(mesh):
    in_specs = (
        P(("grp", "row", "col"), None, None),
        P(("grp", "row", "col")),
        P(("grp", "row", "col")),
        P(("grp", "row", "col")),
        P(("grp", "col")),
        P(("grp", "col")),
        P(("grp", "col")),
        P(("grp", "row")),
        P(("grp", "col")),
        P(("grp", "row")),
        P("grp"),
    )
    out_specs = (
        P(("grp", "col")),
        P(("grp", "row")),
        P(("grp", "row")),
        P(("grp", "col")),
        P("grp"),
    )
    local = functools.partial(body, mesh.shape["row"], mesh.shape["col"])
    return jax.shard_map(local, mesh=mesh, in_specs=in_specs, out_specs=out_specs, check_vma=False)
```
